32 devices in a mesh: ctx: 8 (over y, x, core), tp: 4 (over z).
Axes of the slice: x: 2, y: 2, z: 4, core: 2. Of those that a mesh axis runs over, the one named last changes fastest.
Arguments:
- tokens: bfloat16 [8192, 4096], P('ctx'), may hold values from -6 to 6
- gain: float32 [4096], replicated, may hold values from 0.1 to 1.9
- w_in: bfloat16 [4096, 4096], P(None, 'tp'), may hold values from -0.09375 to 0.09375
- mode_rate: float32 [24, 32], replicated, may hold values from 0.29 to 410, as said below
- mode_coef: float32 [24, 32], replicated, may hold values from -0.2236068 to 0.2236068
- mix: float32 [24, 4096], P(None, 'tp'), may hold values from -1.25 to 1.25
- w_out: bfloat16 [4096, 4096], P('tp'), may hold values from -0.09375 to 0.09375
Outputs:
- out: bfloat16 [8192, 4096], P(('ctx', 'tp'))
The draws below stay inside these ranges and needn't reach their ends.
Inputs may be any that keep to these rules, and one draw needn't show every extreme that they name: `mode_rate`: positive decay rates.
All inputs are finite; a program needn't handle non-finite values.
Results may differ from the reference program's by a relative error of at most 0.012.
Values may be sent and summed in bfloat16 or wider, within the bound.
A program may use at most 128 MiB of HBM per device.

```python
import math
import jax
import jax.numpy as jnp
from jax import lax

D = 4096
K = 24
R = 32
BLOCK = 256
TOK = 1024
TOKENS = 8192
N_TP = 4


def modal_draw(key, slow_share, middle_share):
    key_pick, key_slow, key_middle, key_fast, key_coef = jax.random.split(key, 5)
    grid_shape = (K, R)
    picked = jax.random.uniform(key_pick, grid_shape)
    device_count = TOKENS // TOK
    fast_top = TOKENS / 20.0
    middle_low = 0.15 * device_count
    middle_high = min(20.0 * device_count, fast_top)
    slow_rate = jnp.exp(jax.random.uniform(key_slow, grid_shape, minval=math.log(0.3), maxval=math.log(2.3)))
    middle_rate = jnp.exp(jax.random.uniform(key_middle, grid_shape, minval=math.log(middle_low), maxval=math.log(middle_high)))
    fast_rate = jnp.exp(jax.random.uniform(key_fast, grid_shape, minval=math.log(1.0 / 60.0), maxval=math.log(1.0 / 20.0))) * TOKENS
    rate_value = jnp.where(picked < slow_share, slow_rate, jnp.where(picked < slow_share + middle_share, middle_rate, fast_rate))
    noise = jax.random.truncated_normal(key_coef, -4.0, 4.0, grid_shape)
    coef_value = noise * jnp.sqrt(2.0 * rate_value / TOKENS / R)
    return (rate_value.astype(jnp.float32), coef_value.astype(jnp.float32))


def draw_mode_rate(key, part):
    slow_share = 0.45
    middle_share = 0.3
    rate_value, coef_value = modal_draw(key, slow_share, middle_share)
    return rate_value


def draw_mode_coef(key, part):
    slow_share = 0.45
    middle_share = 0.3
    rate_value, coef_value = modal_draw(key, slow_share, middle_share)
    return coef_value


def block_scale(key, extent, cuts, smallest, top_value):
    def one(axis_at, blocks):
        steps = jax.random.uniform(jax.random.fold_in(jax.random.fold_in(key, 6), axis_at), (blocks,), jnp.float32, smallest / len(cuts), top_value / len(cuts))
        return jnp.repeat(jnp.exp(steps), extent[axis_at] // blocks).reshape((-1,) + (1,) * (len(extent) - axis_at - 1))

    level = one(*cuts[0])
    for cut in cuts[1:]:
        level = level * one(*cut)
    return level


def normal_values(key, extent, spread, limit, cuts=(), kind=jnp.bfloat16):
    factor_of = block_scale(key, extent, cuts, -0.22, 0.18) if cuts else 1.0
    array = jax.random.normal(key, extent, jnp.float32) * spread * factor_of
    return jnp.minimum(jnp.maximum(array, -limit), limit).astype(kind)


def setup_inputs(seed: int = 0) -> dict:
    key_list = jax.random.split(jax.random.key(seed), 8)
    return {
        "tokens": normal_values(key_list[0], (TOKENS, D), 1.0, 6.0, ((0, 8),)),
        "gain": jnp.clip(1.0 + 0.18 * jax.random.normal(key_list[1], (D,), jnp.float32), 0.1, 1.9),
        "w_in": normal_values(key_list[2], (D, D), D ** -0.5, 0.09375, ((1, 4),)),
        "mode_rate": draw_mode_rate(jax.random.fold_in(key_list[7], 71), 0),
        "mode_coef": draw_mode_coef(jax.random.fold_in(key_list[7], 71), 0),
        "mix": normal_values(key_list[5], (K, D), K ** -0.5, 1.25, ((1, 4),), jnp.float32),
        "w_out": normal_values(key_list[6], (D, D), D ** -0.5, 0.09375, ((0, 4),)),
    }


norm_eps = 1e-05

def modal_tables(mode_rate, mode_coef, total_len, block_len):
    filters, mode_count = mode_rate.shape
    log_decay = -mode_rate.astype(jnp.float32) / total_len
    offsets = jnp.arange(block_len, dtype=jnp.float32)
    filter_table = lax.optimization_barrier(jnp.sum(mode_coef[:, :, None] * jnp.exp(log_decay[:, :, None] * offsets[None, None, :]), axis=1)).astype(jnp.bfloat16)
    row_pos = jnp.arange(block_len, dtype=jnp.int32)[:, None]
    col_pos = jnp.arange(block_len, dtype=jnp.int32)[None, :]
    lag_index = jnp.clip(row_pos - col_pos, 0, block_len - 1)
    toeplitz = jnp.where((row_pos >= col_pos)[None], filter_table[:, lag_index], jnp.zeros((), jnp.bfloat16)).astype(jnp.bfloat16)
    flat_decay = log_decay.reshape(-1)
    entry_decay = jnp.exp(flat_decay[None, :] * (offsets[:, None] + 1.0))
    feed_decay = jnp.exp(flat_decay[:, None] * (block_len - 1.0 - offsets)[None, :])
    stride = jnp.exp(flat_decay * block_len)[:, None]
    return (toeplitz.reshape(filters * block_len, block_len), entry_decay, feed_decay, stride)

def block_step(carried, value_block, toeplitz, entry_decay, feed_decay, stride, mix, modal_mix, filters):
    block_len = value_block.shape[0]
    local_terms = jnp.dot(toeplitz, value_block, preferred_element_type=jnp.float32).reshape(filters, block_len, -1)
    mixed_sum = jnp.einsum('kqd,kd->qd', local_terms, mix.astype(jnp.float32))
    carried_terms = jnp.dot(entry_decay, modal_mix * carried, precision=lax.Precision.HIGHEST)
    spectral = (mixed_sum + carried_terms).astype(jnp.bfloat16)
    carried = stride * carried + jnp.dot(feed_decay, value_block.astype(jnp.float32), precision=lax.Precision.HIGHEST)
    return (carried, spectral)

def reference(tokens, gain, w_in, mode_rate, mode_coef, mix, w_out):
    filters, mode_count = mode_rate.shape
    wide_tokens = tokens.astype(jnp.float32)
    row_scale = lax.rsqrt(lax.optimization_barrier(jnp.mean(wide_tokens * wide_tokens, axis=-1, keepdims=True)) + norm_eps)
    normed = (wide_tokens * row_scale * gain.astype(jnp.float32)).astype(jnp.bfloat16)
    values = jnp.dot(normed, w_in, preferred_element_type=jnp.float32).astype(jnp.bfloat16)
    toeplitz, entry_decay, feed_decay, stride = modal_tables(mode_rate, mode_coef, TOKENS, BLOCK)
    modal_mix = (mode_coef[:, :, None] * mix[:, None, :]).reshape(filters * mode_count, -1)
    blocks = values.reshape(TOKENS // BLOCK, BLOCK, D)

    def advance(carried, value_block):
        return block_step(carried, value_block, toeplitz, entry_decay, feed_decay, stride, mix, modal_mix, filters)
    start_state = jnp.zeros((filters * mode_count, D), jnp.float32)
    final_state, pieces = lax.scan(advance, start_state, blocks)
    spectral = pieces.reshape(TOKENS, D)
    group_width = D // N_TP
    total = tokens.astype(jnp.float32)
    for group in range(N_TP):
        partial_value = jnp.dot(spectral[:, group * group_width:(group + 1) * group_width], w_out[group * group_width:(group + 1) * group_width, :], preferred_element_type=jnp.float32)
        partial_value = lax.optimization_barrier(partial_value.astype(jnp.bfloat16)).astype(jnp.float32)
        total = total + partial_value
    return total.astype(jnp.bfloat16)
```

```python
import jax
import jax.numpy as jnp
from jax import lax
from jax.sharding import PartitionSpec as P

BLOCK = 256

norm_eps = 1e-05
F32 = jnp.float32
BF16 = jnp.bfloat16


def dot(a, b):
    return jnp.dot(a, b, preferred_element_type=F32)


def gather_w_out(w_out):
    n_ctx, n_tp = lax.axis_size("ctx"), lax.axis_size("tp")
    rows, width = w_out.shape
    share = rows // n_ctx
    mine = lax.dynamic_slice_in_dim(w_out, lax.axis_index("ctx") * share, share, 0)
    return lax.all_gather(mine, ("tp", "ctx"), tiled=True)


def swap(x, step):
    n = lax.axis_size("ctx")
    return lax.ppermute(x, "ctx", [(i, i ^ step) for i in range(n)])


def incoming_state(summary, log_decay, rows_dev):
    n_ctx = lax.axis_size("ctx")
    place = lax.axis_index("ctx")
    half = summary.shape[1] // 2
    core = place & 1
    total = summary
    prefix = jnp.zeros_like(summary)
    step = 1
    while step < n_ctx:
        if step == 1:
            other = swap(total.astype(BF16), 1)
        else:
            sent = lax.dynamic_slice_in_dim(total, core * half, half, 1).astype(BF16)
            got = swap(sent, step)
            pair = swap(got, 1)
            other = jnp.where(
                core == 0,
                jnp.concatenate([got, pair], axis=1),
                jnp.concatenate([pair, got], axis=1),
            )
        other = other.astype(F32)
        upper = (place & step) != 0
        inner = (place & (step - 1)).astype(F32)
        into = jnp.exp(log_decay * (rows_dev * inner))[:, None]
        across = jnp.exp(log_decay * (rows_dev * float(step)))[:, None]
        prefix = jnp.where(upper, prefix + into * other, prefix)
        if 2 * step < n_ctx:
            total = jnp.where(upper, across * other + total, across * total + other)
        step *= 2
    return prefix


def body(tokens, gain, w_in, mode_rate, mode_coef, mix, w_out):
    rows_dev = tokens.shape[0]
    filters, mode_count = mode_rate.shape
    n_tp = lax.axis_size("tp")
    total_len = rows_dev * lax.axis_size("ctx")
    blocks = rows_dev // BLOCK
    w_all = gather_w_out(w_out)

    wide_tokens = tokens.astype(F32)
    row_scale = lax.rsqrt(jnp.mean(wide_tokens * wide_tokens, axis=-1, keepdims=True) + norm_eps)
    normed = (wide_tokens * row_scale * gain).astype(BF16)
    values = dot(normed, w_in).astype(BF16)
    channels = values.shape[1]

    log_decay = -mode_rate / total_len
    flat_decay = log_decay.reshape(-1)
    offsets = jnp.arange(BLOCK, dtype=F32)
    filter_table = jnp.sum(
        mode_coef[:, :, None] * jnp.exp(log_decay[:, :, None] * offsets[None, None, :]), axis=1
    ).astype(BF16)
    lag_ids = jnp.arange(BLOCK, dtype=jnp.int32)
    lag_grid = (lag_ids[:, None] - lag_ids[None, :]).reshape(1, BLOCK * BLOCK)
    selector = (lag_ids[:, None] == lag_grid).astype(BF16)
    toeplitz = dot(filter_table, selector).astype(BF16).reshape(filters * BLOCK, BLOCK)
    modal_mix = (mode_coef[:, :, None] * mix[:, None, :]).reshape(filters * mode_count, -1)
    positions = jnp.arange(rows_dev, dtype=F32)
    entry_decay = jnp.exp(flat_decay[None, :] * (positions[:, None] + 1.0)).astype(BF16)
    feed_decay = jnp.exp(flat_decay[:, None] * (BLOCK - 1.0 - offsets)[None, :]).astype(BF16)
    tail_decay = jnp.exp(flat_decay[:, None] * (rows_dev - 1.0 - positions)[None, :]).astype(BF16)
    stride = jnp.exp(flat_decay * BLOCK)[:, None]

    summary = dot(tail_decay, values)
    incoming = incoming_state(summary, flat_decay, rows_dev)

    near = []
    carried = None
    for b in range(blocks):
        value_block = values[b * BLOCK : (b + 1) * BLOCK]
        local = dot(toeplitz, value_block).reshape(filters, BLOCK, channels)
        mixed = jnp.einsum("kqd,kd->qd", local, mix)
        if carried is not None:
            mixed = mixed + dot(entry_decay[:BLOCK], (modal_mix * carried).astype(BF16))
        near.append(mixed)
        if b + 1 < blocks:
            fed = dot(feed_decay, value_block)
            carried = fed if carried is None else stride * carried + fed
    near = jnp.concatenate(near, axis=0)
    far = dot(entry_decay, (modal_mix * incoming).astype(BF16))
    spectral = (near + far).astype(BF16)

    mine = lax.all_to_all(spectral, "tp", 0, 1, tiled=True)
    out_rows = rows_dev // n_tp
    residual = lax.dynamic_slice_in_dim(tokens, lax.axis_index("tp") * out_rows, out_rows, 0)
    return (residual.astype(F32) + dot(mine, w_all)).astype(BF16)


def solution(mesh):
    return jax.shard_map(
        body,
        mesh=mesh,
        in_specs=(P("ctx", None), P(), P(None, "tp"), P(), P(), P(None, "tp"), P("tp", None)),
        out_specs=P(("ctx", "tp"), None),
        check_vma=False,
    )
```

```python
import jax
import jax.numpy as jnp
from jax import lax
from jax.sharding import PartitionSpec as P

BLOCK = 256

norm_eps = 1e-05
F32 = jnp.float32
BF16 = jnp.bfloat16


def dot(a, b):
    return jnp.dot(a, b, preferred_element_type=F32)


def tied(x, *after):
    return lax.optimization_barrier((x, *after))[0]


def shift_tp(x, d):
    n = lax.axis_size("tp")
    return lax.ppermute(x, "tp", [(i, (i + d) % n) for i in range(n)])


def swap(x, step):
    n = lax.axis_size("ctx")
    return lax.ppermute(x, "ctx", [(i, i ^ step) for i in range(n)])


def incoming_state(summary, log_decay, rows_dev):
    n_ctx = lax.axis_size("ctx")
    place = lax.axis_index("ctx")
    half = summary.shape[1] // 2
    core = place & 1
    total = summary
    prefix = jnp.zeros_like(summary)
    step = 1
    while step < n_ctx:
        if step == 1:
            other = swap(total.astype(BF16), 1)
        else:
            sent = lax.dynamic_slice_in_dim(total, core * half, half, 1).astype(BF16)
            got = swap(sent, step)
            pair = swap(got, 1)
            other = jnp.where(
                core == 0,
                jnp.concatenate([got, pair], axis=1),
                jnp.concatenate([pair, got], axis=1),
            )
        other = other.astype(F32)
        upper = (place & step) != 0
        inner = (place & (step - 1)).astype(F32)
        into = jnp.exp(log_decay * (rows_dev * inner))[:, None]
        across = jnp.exp(log_decay * (rows_dev * float(step)))[:, None]
        prefix = jnp.where(upper, prefix + into * other, prefix)
        if 2 * step < n_ctx:
            total = jnp.where(upper, across * other + total, across * total + other)
        step *= 2
    return prefix


def body(tokens, gain, w_in, mode_rate, mode_coef, mix, w_out):
    rows_dev = tokens.shape[0]
    filters, mode_count = mode_rate.shape
    n_tp = lax.axis_size("tp")
    total_len = rows_dev * lax.axis_size("ctx")
    blocks = rows_dev // BLOCK
    n_ctx = lax.axis_size("ctx")
    share = w_out.shape[0] // n_ctx
    mine = lax.dynamic_slice_in_dim(w_out, lax.axis_index("ctx") * share, share, 0)
    hops = sorted(range(1, n_tp), key=lambda d: (min(d, n_tp - d), d))
    slabs = {}
    pending = shift_tp(mine, hops[0])

    wide_tokens = tokens.astype(F32)
    row_scale = lax.rsqrt(jnp.mean(wide_tokens * wide_tokens, axis=-1, keepdims=True) + norm_eps)
    normed = (wide_tokens * row_scale * gain).astype(BF16)
    values = dot(normed, w_in).astype(BF16)
    channels = values.shape[1]

    def advance(at, *after):
        nonlocal pending
        if at >= len(hops):
            return
        came = tied(pending, *after)
        slabs[hops[at]] = lax.all_gather(came, "ctx", tiled=True)
        if at + 1 < len(hops):
            pending = shift_tp(tied(mine, came), hops[at + 1])

    advance(0, values)

    log_decay = -mode_rate / total_len
    flat_decay = log_decay.reshape(-1)
    positions = jnp.arange(rows_dev, dtype=F32)
    tail_decay = jnp.exp(flat_decay[:, None] * (rows_dev - 1.0 - positions)[None, :]).astype(BF16)
    summary = dot(tail_decay, values)
    incoming = incoming_state(summary, flat_decay, rows_dev)

    late_coef = tied(mode_coef, summary)
    offsets = jnp.arange(BLOCK, dtype=F32)
    filter_table = jnp.sum(
        late_coef[:, :, None] * jnp.exp(log_decay[:, :, None] * offsets[None, None, :]), axis=1
    ).astype(BF16)
    lag_ids = jnp.arange(BLOCK, dtype=jnp.int32)
    lag_grid = (lag_ids[:, None] - lag_ids[None, :]).reshape(1, BLOCK * BLOCK)
    selector = (lag_ids[:, None] == lag_grid).astype(BF16)
    toeplitz = dot(filter_table, selector).astype(BF16).reshape(filters * BLOCK, BLOCK)
    modal_mix = (mode_coef[:, :, None] * mix[:, None, :]).reshape(filters * mode_count, -1)
    entry_decay = jnp.exp(flat_decay[None, :] * (positions[:, None] + 1.0)).astype(BF16)
    feed_decay = jnp.exp(flat_decay[:, None] * (BLOCK - 1.0 - offsets)[None, :]).astype(BF16)
    stride = jnp.exp(flat_decay * BLOCK)[:, None]

    near = []
    carried = None
    for b in range(blocks):
        value_block = values[b * BLOCK : (b + 1) * BLOCK]
        local = dot(toeplitz, value_block).reshape(filters, BLOCK, channels)
        mixed = jnp.einsum("kqd,kd->qd", local, mix)
        if carried is not None:
            mixed = mixed + dot(entry_decay[:BLOCK], (modal_mix * carried).astype(BF16))
        near.append(mixed)
        if b == 0:
            advance(1, mixed)
        if b == 2:
            advance(2, mixed)
        if b + 1 < blocks:
            fed = dot(feed_decay, value_block)
            carried = fed if carried is None else stride * carried + fed
    near = jnp.concatenate(near, axis=0)
    far = dot(entry_decay, (modal_mix * incoming).astype(BF16))
    spectral = (near + far).astype(BF16)

    for at in range(3, len(hops)):
        advance(at, near)

    out_rows = rows_dev // n_tp
    place = lax.axis_index("tp")

    def rows_of(x, to):
        return lax.dynamic_slice_in_dim(x, lax.rem(to, n_tp) * out_rows, out_rows, 0)

    pieces = {d: shift_tp(rows_of(spectral, place + d), d) for d in hops[::-1]}
    total = rows_of(tokens, place).astype(F32) + dot(rows_of(spectral, place), w_out)
    for d in hops[::-1]:
        total = total + dot(pieces[d], slabs[d])
    return total.astype(BF16)


def solution(mesh):
    return jax.shard_map(
        body,
        mesh=mesh,
        in_specs=(P("ctx", None), P(), P(None, "tp"), P(), P(), P(None, "tp"), P("tp", None)),
        out_specs=P(("ctx", "tp"), None),
        check_vma=False,
    )
```

```python
import jax
import jax.numpy as jnp
from jax import lax
from jax.sharding import PartitionSpec as P

BLOCK = 256

norm_eps = 1e-05
F32 = jnp.float32
BF16 = jnp.bfloat16


def dot(a, b):
    return jnp.dot(a, b, preferred_element_type=F32)


def tied(x, *after):
    return lax.optimization_barrier((x, *after))[0]


def shift_tp(x, d):
    n = lax.axis_size("tp")
    return lax.ppermute(x, "tp", [(i, (i + d) % n) for i in range(n)])


def swap(x, step):
    n = lax.axis_size("ctx")
    return lax.ppermute(x, "ctx", [(i, i ^ step) for i in range(n)])


def incoming_state(summary, log_decay, rows_dev, beside):
    n_ctx = lax.axis_size("ctx")
    place = lax.axis_index("ctx")
    half = summary.shape[1] // 2
    core = place & 1
    total = summary
    prefix = jnp.zeros_like(summary)
    step = 1
    while step < n_ctx:
        if step == 1:
            other = swap(total.astype(BF16), 1)
        else:
            sent = lax.dynamic_slice_in_dim(total, core * half, half, 1).astype(BF16)
            got = tied(swap(sent, step), *beside.get(step, ()))
            pair = swap(got, 1)
            other = jnp.where(
                core == 0,
                jnp.concatenate([got, pair], axis=1),
                jnp.concatenate([pair, got], axis=1),
            )
        other = other.astype(F32)
        upper = (place & step) != 0
        inner = (place & (step - 1)).astype(F32)
        into = jnp.exp(log_decay * (rows_dev * inner))[:, None]
        across = jnp.exp(log_decay * (rows_dev * float(step)))[:, None]
        prefix = jnp.where(upper, prefix + into * other, prefix)
        if 2 * step < n_ctx:
            total = jnp.where(upper, across * other + total, across * total + other)
        step *= 2
    return prefix


def body(tokens, gain, w_in, mode_rate, mode_coef, mix, w_out):
    rows_dev = tokens.shape[0]
    filters, mode_count = mode_rate.shape
    n_tp = lax.axis_size("tp")
    total_len = rows_dev * lax.axis_size("ctx")
    blocks = rows_dev // BLOCK
    n_ctx = lax.axis_size("ctx")
    share = w_out.shape[0] // (n_ctx // 2)
    width = w_out.shape[1] // 2
    chip, core = lax.axis_index("ctx") // 2, lax.axis_index("ctx") & 1
    same_core = [list(range(c, n_ctx, 2)) for c in (0, 1)]
    mine = lax.dynamic_slice(w_out, (chip * share, core * width), (share, width))
    hops = sorted(range(1, n_tp), key=lambda d: (min(d, n_tp - d), d))
    slabs = {}
    shares = {0: mine, n_tp: mine, 1: shift_tp(mine, 1)}

    wide_tokens = tokens.astype(F32)
    row_scale = lax.rsqrt(jnp.mean(wide_tokens * wide_tokens, axis=-1, keepdims=True) + norm_eps)
    normed = (wide_tokens * row_scale * gain).astype(BF16)
    values = dot(normed, w_in).astype(BF16)
    channels = values.shape[1]

    def advance(at, *after):
        if at >= len(hops):
            return
        d = hops[at]
        came = tied(shares[d], *after)
        slabs[d] = lax.all_gather(came, "ctx", axis_index_groups=same_core, tiled=True)
        if at == 0:
            shares[0] = shares[n_tp] = tied(mine, came)
            shares[1] = came
            for e in hops[1:]:
                shares[e] = (
                    shift_tp(shares[e - 1], 1) if 2 * e <= n_tp else shift_tp(shares[e + 1], -1)
                )

    advance(0, values)

    log_decay = -mode_rate / total_len
    flat_decay = log_decay.reshape(-1)
    positions = jnp.arange(rows_dev, dtype=F32)
    tail_decay = jnp.exp(flat_decay[:, None] * (rows_dev - 1.0 - positions)[None, :]).astype(BF16)
    summary = dot(tail_decay, values)
    late_coef = tied(mode_coef, summary, shares[1])
    offsets = jnp.arange(BLOCK, dtype=F32)
    filter_table = jnp.sum(
        late_coef[:, :, None] * jnp.exp(log_decay[:, :, None] * offsets[None, None, :]), axis=1
    ).astype(BF16)
    lag_ids = jnp.arange(BLOCK, dtype=jnp.int32)
    lag_grid = (lag_ids[:, None] - lag_ids[None, :]).reshape(1, BLOCK * BLOCK)
    selector = (lag_ids[:, None] == lag_grid).astype(BF16)
    toeplitz = dot(filter_table, selector).astype(BF16).reshape(filters * BLOCK, BLOCK)
    modal_mix = (mode_coef[:, :, None] * mix[:, None, :]).reshape(filters * mode_count, -1)
    entry_decay = jnp.exp(flat_decay[None, :] * (positions[:, None] + 1.0)).astype(BF16)
    feed_decay = jnp.exp(flat_decay[:, None] * (BLOCK - 1.0 - offsets)[None, :]).astype(BF16)
    stride = jnp.exp(flat_decay * BLOCK)[:, None]

    near = []
    carried = None
    for b in range(blocks):
        value_block = values[b * BLOCK : (b + 1) * BLOCK]
        local = dot(toeplitz, value_block).reshape(filters, BLOCK, channels)
        mixed = jnp.einsum("kqd,kd->qd", local, mix)
        if carried is not None:
            mixed = mixed + dot(entry_decay[:BLOCK], (modal_mix * carried).astype(BF16))
        near.append(mixed)
        if b == 0:
            advance(1, mixed)
        if b == blocks // 2:
            advance(2, mixed)
        if b + 1 < blocks:
            fed = dot(feed_decay, value_block)
            carried = fed if carried is None else stride * carried + fed
    beside = {2: near[: blocks // 2], 4: near[blocks // 2 :]}
    incoming = incoming_state(summary, flat_decay, rows_dev, beside)
    near = jnp.concatenate(near, axis=0)
    far = dot(entry_decay, (modal_mix * incoming).astype(BF16))
    spectral = (near + far).astype(BF16)

    for at in range(3, len(hops)):
        advance(at, near)

    out_rows = rows_dev // n_tp
    place = lax.axis_index("tp")

    def rows_of(x, to):
        return lax.dynamic_slice_in_dim(x, lax.rem(to, n_tp) * out_rows, out_rows, 0)

    def chip_rows(x):
        return jnp.concatenate([x, swap(x, 1)], axis=0)

    pieces = {d: shift_tp(rows_of(spectral, place + d), d) for d in hops[::-1]}
    w_mine = lax.dynamic_slice_in_dim(w_out, core * width, width, 1)
    total = dot(chip_rows(rows_of(spectral, place)), w_mine)
    for d in hops[::-1]:
        total = total + dot(chip_rows(pieces[d]), slabs[d])
    kept = total[:out_rows]
    given = swap(total[out_rows:].astype(BF16), 1).astype(F32)
    summed = jnp.where(
        core == 0,
        jnp.concatenate([kept, given], axis=1),
        jnp.concatenate([given, kept], axis=1),
    )
    return (rows_of(tokens, place).astype(F32) + summed).astype(BF16)


def solution(mesh):
    return jax.shard_map(
        body,
        mesh=mesh,
        in_specs=(P("ctx", None), P(), P(None, "tp"), P(), P(), P(None, "tp"), P("tp", None)),
        out_specs=P(("ctx", "tp"), None),
        check_vma=False,
    )
```

```python
import jax
import jax.numpy as jnp
from jax import lax
from jax.sharding import PartitionSpec as P

BLOCK = 256

norm_eps = 1e-05
F32 = jnp.float32
BF16 = jnp.bfloat16


def dot(a, b):
    return jnp.dot(a, b, preferred_element_type=F32)


def tied(x, *after):
    return lax.optimization_barrier((x, *after))[0]


def shift_tp(x, d):
    n = lax.axis_size("tp")
    return lax.ppermute(x, "tp", [(i, (i + d) % n) for i in range(n)])


def swap(x, step):
    n = lax.axis_size("ctx")
    return lax.ppermute(x, "ctx", [(i, i ^ step) for i in range(n)])


def incoming_state(summary, first, log_decay, rows_dev, beside):
    n_ctx = lax.axis_size("ctx")
    place = lax.axis_index("ctx")
    half = summary.shape[1] // 2
    core = place & 1
    total = summary
    prefix = jnp.zeros_like(summary)
    step = 1
    while step < n_ctx:
        if step == 1:
            other = first
        else:
            sent = lax.dynamic_slice_in_dim(total, core * half, half, 1).astype(BF16)
            got = tied(swap(sent, step), *beside.get(step, ()))
            pair = swap(got, 1)
            other = jnp.where(
                core == 0,
                jnp.concatenate([got, pair], axis=1),
                jnp.concatenate([pair, got], axis=1),
            )
        other = other.astype(F32)
        upper = (place & step) != 0
        inner = (place & (step - 1)).astype(F32)
        into = jnp.exp(log_decay * (rows_dev * inner))[:, None]
        across = jnp.exp(log_decay * (rows_dev * float(step)))[:, None]
        prefix = jnp.where(upper, prefix + into * other, prefix)
        if 2 * step < n_ctx:
            total = jnp.where(upper, across * other + total, across * total + other)
        step *= 2
    return prefix


def body(tokens, gain, w_in, mode_rate, mode_coef, mix, w_out):
    rows_dev = tokens.shape[0]
    filters, mode_count = mode_rate.shape
    n_tp = lax.axis_size("tp")
    total_len = rows_dev * lax.axis_size("ctx")
    blocks = rows_dev // BLOCK
    n_ctx = lax.axis_size("ctx")
    share = w_out.shape[0] // (n_ctx // 2)
    width = w_out.shape[1] // 2
    chip, core = lax.axis_index("ctx") // 2, lax.axis_index("ctx") & 1
    same_core = [list(range(c, n_ctx, 2)) for c in (0, 1)]
    mine = lax.dynamic_slice(w_out, (chip * share, core * width), (share, width))
    hops = sorted(range(1, n_tp), key=lambda d: (min(d, n_tp - d), d))
    slabs = {}
    shares = {0: mine, n_tp: mine, 1: shift_tp(mine, 1)}

    wide_tokens = tokens.astype(F32)
    row_scale = lax.rsqrt(jnp.mean(wide_tokens * wide_tokens, axis=-1, keepdims=True) + norm_eps)
    normed = (wide_tokens * row_scale * gain).astype(BF16)
    values = dot(normed, w_in).astype(BF16)
    channels = values.shape[1]

    def advance(at, *after):
        if at >= len(hops):
            return
        d = hops[at]
        came = tied(shares[d], *after)
        slabs[d] = lax.all_gather(came, "ctx", axis_index_groups=same_core, tiled=True)
        if at == 0:
            shares[0] = shares[n_tp] = tied(mine, came)
            shares[1] = came
            for e in hops[1:]:
                shares[e] = (
                    shift_tp(shares[e - 1], 1) if 2 * e <= n_tp else shift_tp(shares[e + 1], -1)
                )

    advance(0, values)

    log_decay = -mode_rate / total_len
    flat_decay = log_decay.reshape(-1)
    positions = jnp.arange(rows_dev, dtype=F32)
    tail_decay = jnp.exp(flat_decay[:, None] * (rows_dev - 1.0 - positions)[None, :]).astype(BF16)
    summary = dot(tail_decay, values)
    first = swap(summary.astype(BF16), 1)
    late_coef = tied(mode_coef, first, shares[1])
    offsets = jnp.arange(BLOCK, dtype=F32)
    filter_table = jnp.sum(
        late_coef[:, :, None] * jnp.exp(log_decay[:, :, None] * offsets[None, None, :]), axis=1
    ).astype(BF16)
    lag_ids = jnp.arange(BLOCK, dtype=jnp.int32)
    lag_grid = (lag_ids[:, None] - lag_ids[None, :]).reshape(1, BLOCK * BLOCK)
    selector = (lag_ids[:, None] == lag_grid).astype(BF16)
    toeplitz = dot(filter_table, selector).astype(BF16).reshape(filters * BLOCK, BLOCK)
    modal_mix = (mode_coef[:, :, None] * mix[:, None, :]).reshape(filters * mode_count, -1)
    entry_decay = jnp.exp(flat_decay[None, :] * (positions[:, None] + 1.0)).astype(BF16)
    feed_decay = jnp.exp(flat_decay[:, None] * (BLOCK - 1.0 - offsets)[None, :]).astype(BF16)
    stride = jnp.exp(flat_decay * BLOCK)[:, None]

    near = []
    carried = None
    for b in range(blocks):
        value_block = values[b * BLOCK : (b + 1) * BLOCK]
        local = dot(toeplitz, value_block).reshape(filters, BLOCK, channels)
        mixed = jnp.einsum("kqd,kd->qd", local, mix)
        if carried is not None:
            mixed = mixed + dot(entry_decay[:BLOCK], (modal_mix * carried).astype(BF16))
        near.append(mixed)
        if b == 0:
            advance(1, mixed)
        if b == blocks // 2:
            advance(2, mixed)
        if b + 1 < blocks:
            fed = dot(feed_decay, value_block)
            carried = fed if carried is None else stride * carried + fed
    beside = {2: near[:1], 4: near[1:3]}
    incoming = incoming_state(summary, first, flat_decay, rows_dev, beside)
    near = jnp.concatenate(near, axis=0)
    far = dot(entry_decay, (modal_mix * incoming).astype(BF16))
    spectral = (near + far).astype(BF16)

    for at in range(3, len(hops)):
        advance(at, near)

    out_rows = rows_dev // n_tp
    place = lax.axis_index("tp")

    def rows_of(x, to):
        return lax.dynamic_slice_in_dim(x, lax.rem(to, n_tp) * out_rows, out_rows, 0)

    def chip_rows(x):
        return jnp.concatenate([x, swap(x, 1)], axis=0)

    pieces = {d: shift_tp(rows_of(spectral, place + d), d) for d in hops}
    w_mine = lax.dynamic_slice_in_dim(w_out, core * width, width, 1)
    total = dot(chip_rows(rows_of(spectral, place)), w_mine)
    for d in hops:
        total = total + dot(chip_rows(tied(pieces[d], total)), slabs[d])
    kept = total[:out_rows]
    given = swap(total[out_rows:].astype(BF16), 1).astype(F32)
    summed = jnp.where(
        core == 0,
        jnp.concatenate([kept, given], axis=1),
        jnp.concatenate([given, kept], axis=1),
    )
    return (rows_of(tokens, place).astype(F32) + summed).astype(BF16)


def solution(mesh):
    return jax.shard_map(
        body,
        mesh=mesh,
        in_specs=(P("ctx", None), P(), P(None, "tp"), P(), P(), P(None, "tp"), P("tp", None)),
        out_specs=P(("ctx", "tp"), None),
        check_vma=False,
    )
```
